512 devices in a mesh: dp: 64 (over y, z_lo, core), mp: 8 (over x, z_hi).
Axes of the slice: x: 4, y: 8, z: 8 (z_hi: 2, z_lo: 4; z = z_hi * 4 + z_lo), core: 2. Of those that a mesh axis runs over, the one named last changes fastest.
Arguments:
- context: bfloat16 [65536, 4096], P('dp', 'mp'), may hold values from -6 to 6
- w_out: bfloat16 [4096, 4096], P('dp', 'mp'), may hold values from -0.09375 to 0.09375
- residual: bfloat16 [65536, 4096], P('dp', 'mp'), may hold values from -6 to 6
- w_proj: bfloat16 [3584, 4096], P('dp', 'mp'), may hold values from -0.09375 to 0.09375
- hidden: bfloat16 [65536, 3584], P(('dp', 'mp')), may hold values from -6 to 6
- gain: float32 [3584], replicated, may hold values from 0.25 to 1.75
- matched: int32 [24576], P('dp'), may hold values from 0 to 1023, as said below
Outputs:
- grad_hidden: bfloat16 [65536, 3584], P(('dp', 'mp'))
- gain_update: float32 [3584], replicated
The draws below stay inside these ranges and needn't reach their ends.
Inputs may be any that keep to these rules, and one draw needn't show every extreme that they name: Within a token group the entries are distinct; split a group's 1024 tokens into 8 equal consecutive blocks: each block holds exactly 384 / 8 matched tokens, listed block after block, ascending within a block.
All inputs are finite; a program needn't handle non-finite values.
Results may differ from the reference program's by a relative error of at most 0.018.
Values may be sent and summed in bfloat16 or wider, within the bound.
No kernel may reach another device: no remote copies, remote signals or barrier semaphores. Data moves between devices by JAX's collectives and lax.ppermute only.
A program may use at most 64 MiB of HBM per device.

```python
import jax
import jax.numpy as jnp
from jax import lax

DS = 3584
TWIN = 4096
TCTX = 4096
TOK_DP = 1024
MATCH = 384
TOKENS = 65536
N_DP = 64
N_MP = 8


def draw_matched(key, part):
    key = jax.random.fold_in(key, 7)
    blocks = N_DP * N_MP
    sub = TOK_DP // N_MP
    pick = MATCH // N_MP
    keys = jax.random.split(key, blocks)
    perms = jax.vmap(lambda one_key: jax.random.permutation(one_key, sub))(keys)[:, :pick]
    chosen = jnp.sort(perms.astype(jnp.int32), axis=1)
    owner = jnp.arange(blocks, dtype=jnp.int32) % N_MP
    column = jnp.arange(pick, dtype=jnp.int32)
    chosen = jnp.where((owner[:, None] == 0) & (column[None, :] == 0), 0, chosen)
    chosen = jnp.where((owner[:, None] == N_MP - 1) & (column[None, :] == pick - 1), sub - 1, chosen)
    return (chosen + owner[:, None] * sub).reshape(-1).astype(jnp.int32)


def steps_of(own_key, dims, pieces, least, high):
    level = 1.0
    for dim, shards_of in pieces:
        draws = jax.random.uniform(jax.random.fold_in(jax.random.fold_in(own_key, 6), dim), (shards_of,), jnp.float32, least / len(pieces), high / len(pieces))
        level = level * jnp.repeat(jnp.exp(draws), dims[dim] // shards_of).reshape((-1,) + (1,) * (len(dims) - 1 - dim))
    return level


def noise(own_key, dims, scale, most, pieces=(), kind=jnp.bfloat16):
    factor_of = steps_of(own_key, dims, pieces, -0.22, 0.18) if pieces else 1.0
    drawn = jax.random.normal(own_key, dims, jnp.float32) * scale * factor_of
    return jnp.minimum(jnp.maximum(drawn, -most), most).astype(kind)


def setup_inputs(seed: int = 0) -> dict:
    key_list = jax.random.split(jax.random.key(seed), 8)
    return {
        "context": noise(key_list[0], (TOKENS, TCTX), 1.0, 6.0, ((0, 64), (1, 8))),
        "w_out": noise(key_list[1], (TCTX, TWIN), TCTX ** -0.5, 0.09375, ((0, 64), (1, 8))),
        "residual": noise(key_list[2], (TOKENS, TWIN), 1.0, 6.0, ((0, 64), (1, 8))),
        "w_proj": noise(key_list[3], (DS, TWIN), DS ** -0.5, 0.09375, ((0, 64), (1, 8))),
        "hidden": noise(key_list[4], (TOKENS, DS), 1.0, 6.0, ((0, 512),)),
        "gain": jnp.clip(1.0 + 0.15 * jax.random.normal(key_list[5], (DS,), jnp.float32), 0.25, 1.75),
        "matched": draw_matched(jax.random.fold_in(key_list[7], 71), 0),
    }


EPS = 1e-06

def reference(context, w_out, residual, w_proj, hidden, gain, matched):
    groups = jnp.arange(N_DP, dtype=jnp.int32)[:, None] * TOK_DP
    rows = (matched.reshape(N_DP, MATCH).astype(jnp.int32) + groups).reshape(-1).astype(jnp.int32)
    teacher = residual[rows].astype(jnp.float32) + jnp.dot(context[rows], w_out, preferred_element_type=jnp.float32)
    hid = hidden[rows].astype(jnp.float32)
    stat = lax.rsqrt(lax.optimization_barrier(jnp.mean(hid * hid, axis=-1, keepdims=True)) + EPS)
    normed = (hid * stat * gain).astype(jnp.bfloat16)
    pred = jnp.dot(normed, w_proj, preferred_element_type=jnp.float32)
    g_pred = (pred - teacher).astype(jnp.bfloat16)
    block = TWIN // N_MP
    g_normed = jnp.zeros((rows.shape[0], DS), jnp.float32)
    for index in range(N_MP):
        piece = g_pred[:, index * block:(index + 1) * block]
        weights = w_proj[:, index * block:(index + 1) * block]
        part = jnp.dot(piece, weights.T, preferred_element_type=jnp.float32).astype(jnp.bfloat16)
        g_normed = g_normed + part.astype(jnp.float32)
    scaled = g_normed * gain
    inner = lax.optimization_barrier(jnp.sum(hid * scaled, axis=-1, keepdims=True))
    grad_rows = (stat * scaled - hid * stat * stat * stat * inner / DS).astype(jnp.bfloat16)
    grad_hidden = jnp.zeros((TOKENS, DS), jnp.bfloat16).at[rows].set(grad_rows)
    grad_gain = lax.optimization_barrier(jnp.sum(g_normed * hid * stat, axis=0))
    gain_update = grad_gain * lax.rsqrt(jnp.mean(grad_gain * grad_gain) + EPS)
    return (grad_hidden, gain_update)
```

```python
import jax
import jax.numpy as jnp
from jax import lax
from jax.experimental import pallas as pl
from jax.experimental.pallas import tpu as pltpu
from jax.sharding import Mesh
from jax.sharding import PartitionSpec as P

EPS = 1e-06
NY, NZL, NC, NX, NZH = 8, 4, 2, 4, 2
NZ = NZL * NZH
AXES = ("y", "zl", "c", "x", "zh")
F32 = jnp.float32
BF16 = jnp.bfloat16


def dev(y, z, c, x):
    return (((y * NZL + z % NZL) * NC + c) * NX + x) * NZH + z // NZL


CHIPS = [(y, z, x) for y in range(NY) for z in range(NZ) for x in range(NX)]


def moved(step):
    pairs = []
    for y, z, x in CHIPS:
        pairs.append((dev(y, z, 0, x), dev((y + step) % NY, z, 0, x)))
        pairs.append((dev(y, z, 1, x), dev(y, (z + step) % NZ, 1, x)))
    return pairs


FORTH, BACK = moved(1), moved(-1)
LINES = [[dev(y, z, 0, x) for z in range(NZ)] for y in range(NY) for x in range(NX)] + [
    [dev(y, z, 1, x) for y in range(NY)] for z in range(NZ) for x in range(NX)
]
FIRST = [
    [dev(h * 4 + y, z, c, x) for c in range(NC) for x in range(NX) for y in range(4)]
    for h in range(2)
    for z in range(NZ)
]
SECOND = [
    [dev(h * 4 + y, z, c, x) for h in range(2) for z in range(NZ)]
    for c in range(NC)
    for x in range(NX)
    for y in range(4)
]


def ring(block):
    held = {0: block}
    ahead = behind = block
    for s in range(1, 4):
        behind = lax.ppermute(behind, AXES, FORTH)
        ahead = lax.ppermute(ahead, AXES, BACK)
        held[8 - s], held[s] = behind, ahead
    half = block.shape[0] // 2
    low = lax.ppermute(behind[:half], AXES, FORTH)
    high = lax.ppermute(ahead[half:], AXES, BACK)
    held[4] = jnp.concatenate([low, high], axis=0)
    return [held[k] for k in range(8)]


def load_all(blocks, wbuf, sems):
    for k, block in enumerate(blocks):
        pltpu.make_async_copy(block, wbuf.at[k], sems.at[k]).start()


def forward_kernel(meta, a_ref, *refs):
    blocks, (out, wbuf, sems) = refs[:8], refs[8:]
    load_all(blocks, wbuf, sems)
    core, z = meta[0], meta[1]
    out[...] = jnp.zeros_like(out)

    def step(k, carry):
        pltpu.make_async_copy(blocks[0], wbuf.at[k], sems.at[k]).wait()

        @pl.when(core == 0)
        def _():
            lanes = pl.ds(pl.multiple_of((k % 2) * 512, 512), 512)
            for g in range(2):
                a = a_ref[g, k // 2, :, lanes]
                for h in range(2):
                    out[g, :, h * 512 : h * 512 + 512] += jnp.dot(
                        a, wbuf[k, h * 512 : h * 512 + 512, :], preferred_element_type=F32
                    )

        @pl.when(core == 1)
        def _():
            zk = (z + k) % NZ
            to = pl.ds(pl.multiple_of((zk // NZL) * 512, 512), 512)
            for g in range(2):
                a = jnp.concatenate(
                    [
                        a_ref[g, x, :, pl.ds(pl.multiple_of(h * 512 + (zk % NZL) * 128, 128), 128)]
                        for x in range(NX)
                        for h in range(NZH)
                    ],
                    axis=1,
                )
                out[g, :, to] += jnp.dot(a, wbuf[k], preferred_element_type=F32)

        return carry

    lax.fori_loop(0, 8, step, 0)


def backward_kernel(a_ref, pred, att, res, *refs):
    blocks, (out, gain_out, g_buf, wbuf, sems) = refs[:8], refs[8:]
    load_all(blocks, wbuf, sems)
    for g in range(2):
        g_buf[g] = (pred[g] - (res[g].astype(F32) + att[1 - g])).astype(BF16)
    nt = (((1,), (1,)), ((), ()))
    for k in range(8):
        pltpu.make_async_copy(blocks[k], wbuf.at[k], sems.at[k]).wait()
        total = jnp.zeros((1, 512), F32)
        for g in range(2):
            term = lax.dot_general(
                g_buf[g, :, :512], wbuf[k, :512, :], nt, preferred_element_type=F32
            ) + lax.dot_general(g_buf[g, :, 512:], wbuf[k, 512:, :], nt, preferred_element_type=F32)
            out[g, :, k * 448 : k * 448 + 448] = term.astype(BF16)[:, :448]
            a = a_ref[g, k // 2, :, (k % 2) * 512 : (k % 2) * 512 + 512].astype(F32)
            total = total + jnp.sum(term * a, axis=0, keepdims=True)
        gain_out[k : k + 1, :] = total


VMEM = pl.BlockSpec(memory_space=pltpu.VMEM)
SMEM = pl.BlockSpec(memory_space=pltpu.SMEM)
ANY = pl.BlockSpec(memory_space=pl.ANY)
PARAMS = pltpu.CompilerParams(vmem_limit_bytes=48 * 1024 * 1024)


def forward(meta, acts, blocks):
    return pl.pallas_call(
        forward_kernel,
        out_shape=jax.ShapeDtypeStruct((2, 192, 1024), F32),
        in_specs=[SMEM, VMEM] + [ANY] * 8,
        out_specs=VMEM,
        scratch_shapes=[pltpu.VMEM((8, 1024, 512), BF16), pltpu.SemaphoreType.DMA((8,))],
        compiler_params=PARAMS,
        cost_estimate=pl.CostEstimate(flops=2 * 384 * 4096 * 1024, bytes_accessed=13 << 20, transcendentals=0),
        name="forward",
    )(meta, acts, *blocks)


def backward(acts, pred, att, res, blocks):
    return pl.pallas_call(
        backward_kernel,
        out_shape=(
            jax.ShapeDtypeStruct((2, 192, 3584), BF16),
            jax.ShapeDtypeStruct((8, 512), F32),
        ),
        in_specs=[VMEM] * 4 + [ANY] * 8,
        out_specs=(VMEM, VMEM),
        scratch_shapes=[
            pltpu.VMEM((2, 192, 1024), BF16),
            pltpu.VMEM((8, 1024, 512), BF16),
            pltpu.SemaphoreType.DMA((8,)),
        ],
        compiler_params=PARAMS,
        cost_estimate=pl.CostEstimate(flops=2 * 384 * 4096 * 1024, bytes_accessed=16 << 20, transcendentals=0),
        name="backward",
    )(acts, pred, att, res, *blocks)


def swapped(pairs):
    return [(dev(y, z, a, x), dev(y, z, b, x)) for y, z, x in CHIPS for a, b in pairs]


def body(context, w_out, residual, w_proj, hidden, gain, matched):
    width = hidden.shape[1]
    own_rows = hidden.shape[0]
    y, c, x, zh = (lax.axis_index(name) for name in ("y", "c", "x", "zh"))
    z = zh * NZL + lax.axis_index("zl")
    first = c == 0

    proj = jnp.pad(w_proj, ((0, 8), (0, 0)))
    got = lax.ppermute(jnp.where(first, w_out, proj), AXES, swapped([(0, 1), (1, 0)]))
    kept = jnp.where(first, proj, w_out)
    pair = jnp.stack([jnp.where(first, kept, got), jnp.where(first, got, kept)])

    blocks = matched.reshape(NX, NZH, 48)
    picks = blocks.transpose(1, 0, 2).reshape(NZH, 192)
    mine = lax.dynamic_index_in_dim(picks, zh, 0, keepdims=False)
    theirs = lax.dynamic_index_in_dim(picks, 1 - zh, 0, keepdims=False)
    away = jnp.concatenate([context[theirs], residual[theirs]], axis=1)
    other = lax.ppermute(away, "zh", [(0, 1), (1, 0)])

    local = lax.dynamic_slice_in_dim(mine, x * 48, 48, 0) - (x * NZH + zh) * own_rows
    hid = hidden[local].astype(F32)
    stat = lax.rsqrt(jnp.mean(hid * hid, axis=-1, keepdims=True) + EPS)
    normed = (hid * stat * gain).astype(BF16).reshape(48, 8, 448)
    normed = jnp.roll(jnp.pad(normed, ((0, 0), (0, 0), (0, 64))), -y, axis=1).reshape(48, 4096)
    normed_all = lax.all_gather(normed, "x", axis=0, tiled=True)

    here = jnp.concatenate([context[mine], residual[mine]], axis=1)
    low = jnp.where(zh == 0, here, other)
    high = jnp.where(zh == 0, other, here)
    heads = jnp.concatenate([low[:, :512], high[:, :512]], axis=1)
    res = jnp.concatenate([low[:, 512:], high[:, 512:]], axis=1)
    heads_all = lax.all_gather(heads, "x", axis=0)
    res_both = jnp.stack([res, lax.ppermute(res, AXES, swapped([(1, 0)]))])

    lines = lax.all_to_all(
        jnp.broadcast_to(pair.reshape(1, 128, 512), (8, 128, 512)), AXES, 0, 0, axis_index_groups=LINES
    )
    tight = jnp.pad(lines.reshape(2, 8, 64, 512)[:, :, :56].reshape(2, 448, 512), ((0, 0), (0, 64), (0, 0)))
    line = jnp.where(first, tight.reshape(1024, 512), lines.reshape(1024, 512))
    held = ring(line)

    normed_all = normed_all.reshape(192, 4, 1024).transpose(1, 0, 2)
    keep = jnp.where(first, normed_all, heads_all)
    give = jnp.where(first, heads_all, normed_all)
    acts = jnp.stack([keep, lax.ppermute(give, AXES, swapped([(0, 1), (1, 0)]))])

    meta = jnp.stack([c, z]).astype(jnp.int32)
    product = forward(meta, acts, held)
    att = lax.ppermute(product, AXES, swapped([(1, 0)]))
    term, gain_rel = backward(acts, product, att, res_both, held)

    term = term.reshape(2, NX, 48, width)
    total = None
    for d in range(1, NX):
        part = lax.dynamic_index_in_dim(term, (x + d) % NX, 1, keepdims=False)
        pairs = [(dev(yy, zz, 0, xx), dev(yy, zz, 0, (xx + d) % NX)) for yy, zz, xx in CHIPS]
        part = lax.ppermute(part, AXES, pairs).astype(F32)
        total = part if total is None else total + part
    total = total + lax.dynamic_index_in_dim(term, x, 1, keepdims=False).astype(F32)
    handed = lax.ppermute(total[1].astype(BF16), AXES, swapped([(0, 1)]))
    g_normed = jnp.where(first, total[0], handed.astype(F32))
    g_normed = jnp.roll(g_normed.reshape(48, 8, 448), y, axis=1).reshape(48, width)

    gain_nat = jnp.roll(gain_rel[:, :448], y, axis=0).reshape(width) / gain
    gain_nat = jnp.where(first, gain_nat, 0.0).reshape(28, 128)
    gathered = lax.all_to_all(
        jnp.broadcast_to(gain_nat[None], (32, 28, 128)), AXES, 0, 0, axis_index_groups=FIRST
    )
    gain_nat = jnp.sum(gathered, axis=0)
    gathered = lax.all_to_all(
        jnp.broadcast_to(gain_nat[None], (16, 28, 128)), AXES, 0, 0, axis_index_groups=SECOND
    )
    grad_gain = jnp.sum(gathered, axis=0).reshape(width)
    gain_update = grad_gain * lax.rsqrt(jnp.mean(grad_gain * grad_gain) + EPS)

    scaled = g_normed * gain
    inner = jnp.sum(hid * scaled, axis=-1, keepdims=True)
    grad_rows = (stat * scaled - hid * stat * stat * stat * inner / width).astype(BF16)
    grad_hidden = jnp.zeros((own_rows, width), BF16).at[local].set(grad_rows)
    return (grad_hidden, gain_update)


def solution(mesh):
    fine = Mesh(mesh.devices.reshape(NY, NZL, NC, NX, NZH), AXES)
    dp, mp = ("y", "zl", "c"), ("x", "zh")
    return jax.shard_map(
        body,
        mesh=fine,
        in_specs=(P(dp, mp), P(dp, mp), P(dp, mp), P(dp, mp), P(dp + mp, None), P(), P(dp)),
        out_specs=(P(dp + mp, None), P()),
        check_vma=False,
    )
```

```python
import jax
import jax.numpy as jnp
from jax import lax
from jax.experimental import pallas as pl
from jax.experimental.pallas import tpu as pltpu
from jax.sharding import Mesh
from jax.sharding import PartitionSpec as P

EPS = 1e-06
NY, NZL, NC, NX, NZH = 8, 4, 2, 4, 2
NZ = NZL * NZH
AXES = ("y", "zl", "c", "x", "zh")
F32 = jnp.float32
BF16 = jnp.bfloat16
NT = (((1,), (1,)), ((), ()))


def dev(y, z, c, x):
    return (((y * NZL + z % NZL) * NC + c) * NX + x) * NZH + z // NZL


CHIPS = [(y, z, x) for y in range(NY) for z in range(NZ) for x in range(NX)]
Z_ON_0 = [[dev(y, z, 0, x) for z in range(NZ)] for y in range(NY) for x in range(NX)] + [
    [dev(y, z, 1, x) for y in range(NY)] for z in range(NZ) for x in range(NX)
]
Y_ON_0 = [[dev(y, z, 0, x) for y in range(NY)] for z in range(NZ) for x in range(NX)] + [
    [dev(y, z, 1, x) for z in range(NZ)] for y in range(NY) for x in range(NX)
]
FIRST = [
    [dev(h * 4 + y, z, c, x) for x in range(NX) for y in range(4)]
    for h in range(2)
    for z in range(NZ)
    for c in range(NC)
]
SECOND = [
    [dev(h * 4 + y, z, c, x) for h in range(2) for z in range(NZ)]
    for c in range(NC)
    for x in range(NX)
    for y in range(4)
]
SWAP = [(0, 1), (1, 0)]

VMEM = pl.BlockSpec(memory_space=pltpu.VMEM)
SMEM = pl.BlockSpec(memory_space=pltpu.SMEM)
ANY = pl.BlockSpec(memory_space=pl.ANY)
PARAMS = pltpu.CompilerParams(vmem_limit_bytes=48 * 1024 * 1024)


def call(kernel, outs, ins, scratch, flops, nbytes, name):
    return pl.pallas_call(
        kernel,
        out_shape=[jax.ShapeDtypeStruct(shape, kind) for shape, kind in outs],
        in_specs=ins,
        out_specs=[VMEM] * len(outs),
        scratch_shapes=scratch,
        compiler_params=PARAMS,
        cost_estimate=pl.CostEstimate(flops=flops, bytes_accessed=nbytes, transcendentals=0),
        name=name,
    )


def hot_rows(idx, b):
    return (lax.broadcasted_iota(jnp.int32, (48, 128), 1) + b * 128 == idx[b]).astype(BF16)


def pick_rows(meta, idx, context, residual, mine, theirs):
    for b in range(8):
        x, zh = b // NZH, b % NZH
        hot = hot_rows(idx, b)
        for part, ref in enumerate((context, residual)):
            rows = jnp.dot(hot, ref[b * 128 : b * 128 + 128, :], preferred_element_type=F32).astype(BF16)
            at = (slice(x * 48, x * 48 + 48), slice(part * 512, part * 512 + 512))

            @pl.when(meta[1] == zh)
            def _():
                mine[at] = rows

            @pl.when(meta[1] != zh)
            def _():
                theirs[at] = rows


def norm_rows(meta, idx, hidden, gain, hid_out, normed_out):
    hid = jnp.dot(hot_rows(idx, meta[2]), hidden[...], preferred_element_type=F32)
    hid_out[...] = hid.astype(BF16)
    stat = lax.rsqrt(jnp.mean(hid * hid, axis=1, keepdims=True) + EPS)
    normed_out[...] = (hid * stat * gain[...]).astype(BF16)


def pair_rows(meta, got, proj, outp, out):
    @pl.when(meta[3] == 0)
    def _():
        for i in range(8):
            out[i, 0, :56, :] = proj[...]
            out[i, 0, 56:, :] = jnp.zeros((8, 512), BF16)
            out[i, 1] = got[...]

    @pl.when(meta[3] != 0)
    def _():
        for i in range(8):
            out[i, 0] = got[...]
            out[i, 1] = outp[...]


def tighten(meta, lines, out):
    @pl.when(meta[3] == 0)
    def _():
        for h in range(NZH):
            for i in range(8):
                row = h * 512 + i * 56
                out[row : row + 56, :] = lines[h * 4 + i // 2, i % 2, :56, :]
            out[h * 512 + 448 : h * 512 + 512, :] = jnp.zeros((64, 512), BF16)

    @pl.when(meta[3] != 0)
    def _():
        for i in range(16):
            out[i * 64 : i * 64 + 64, :] = lines[i // 2, i % 2]


def join(meta, here, other, heads, res):
    def put(zh, low, high):
        @pl.when(meta[1] == zh)
        def _():
            heads[:, :512], heads[:, 512:] = low[:, :512], high[:, :512]
            res[:, :512], res[:, 512:] = low[:, 512:], high[:, 512:]

    put(0, here, other)
    put(1, other, here)


def choose(meta, *refs):
    normed, heads, (keep, give) = refs[0], refs[1 : 1 + NX], refs[1 + NX :]

    def put(core, to_normed, to_heads):
        @pl.when(meta[3] == core)
        def _():
            for y in range(NY):
                to_normed[:, y * 512 : y * 512 + 448] = normed[:, y * 448 : y * 448 + 448]
                to_normed[:, y * 512 + 448 : y * 512 + 512] = jnp.zeros((192, 64), BF16)
            for d in range(NX):
                x = (meta[4] + d) % NX
                to_heads[:, pl.ds(pl.multiple_of(x * 1024, 1024), 1024)] = heads[d][...]

    put(0, keep, give)
    put(1, give, keep)


def load(w, buf, sems):
    copies = [pltpu.make_async_copy(w.at[k], buf.at[k], sems.at[k]) for k in range(8)]
    for copy in copies:
        copy.start()
    return copies


def forward(meta, own, oth, w, out, teach, buf, sems):
    copies = load(w, buf, sems)
    out[...] = jnp.zeros_like(out)

    def part(lanes):
        pieces = [jnp.concatenate([ref[:, lane] for lane in lanes], axis=1) for ref in (own, oth)]
        return jnp.concatenate(pieces, axis=0)

    for k in range(8):
        copies[k].wait()

        @pl.when(meta[3] == 0)
        def _():
            a = part([slice(k * 512, k * 512 + 512)])
            for h in range(NZH):
                cols = slice(h * 512, h * 512 + 512)
                out[:, cols] += jnp.dot(a, buf[k, cols, :], preferred_element_type=F32)

        @pl.when(meta[3] != 0)
        def _():
            a = part([slice(y * 512 + k % NZL * 128, y * 512 + k % NZL * 128 + 128) for y in range(NY)])
            cols = slice(k // NZL * 512, k // NZL * 512 + 512)
            out[:, cols] += jnp.dot(a, buf[k], preferred_element_type=F32)

    teach[:192] = out[192:].astype(BF16)
    teach[192:] = out[:192].astype(BF16)


def backward(meta, pred, teach, res_own, res_oth, own, oth, gain, w, term_own, term_oth, gain_out, g_buf, buf, sems):
    copies = load(w, buf, sems)
    g_buf[:192] = (pred[:192] - (res_own[...].astype(F32) + teach[:192].astype(F32))).astype(BF16)
    g_buf[192:] = (pred[192:] - (res_oth[...].astype(F32) + teach[192:].astype(F32))).astype(BF16)
    for y in range(NY):
        copies[y].wait()
        cols = slice(y * 448, y * 448 + 448)
        lanes = slice(y * 512, y * 512 + 448)
        term = lax.dot_general(g_buf[:, :512], buf[y, :448, :], NT, preferred_element_type=F32)
        term = term + lax.dot_general(g_buf[:, 512:], buf[y, 512:960, :], NT, preferred_element_type=F32)
        a = jnp.concatenate([own[:, lanes], oth[:, lanes]], axis=0).astype(F32)
        total = jnp.sum(term * a, axis=0, keepdims=True) / gain[:, cols]
        gain_out[:, cols] = jnp.where(meta[3] == 0, total, 0.0)
        term = term.astype(BF16)
        term_own[:, cols] = term[:192]
        term_oth[:, cols] = term[192:]


def finish(meta, idx, part0, part1, part2, part3, hid_ref, gain_ref, out):
    gain = gain_ref[...]
    hid = hid_ref[...].astype(F32)
    scaled = (part0[...].astype(F32) + part1[...].astype(F32)) + (part2[...].astype(F32) + part3[...].astype(F32))
    scaled = scaled * gain
    width = hid.shape[1]
    stat = lax.rsqrt(jnp.mean(hid * hid, axis=1, keepdims=True) + EPS)
    inner = jnp.sum(hid * scaled, axis=1, keepdims=True)
    rows = (stat * scaled - hid * (stat * stat * stat * inner / width)).astype(BF16)
    m = meta[2]
    own = idx[:, :48]
    for b in range(1, 8):
        own = jnp.where(m == b, idx[:, b * 48 : b * 48 + 48] - b * 128, own)
    hot = (lax.broadcasted_iota(jnp.int32, (128, 48), 0) == own).astype(BF16)
    out[...] = jnp.dot(hot, rows, preferred_element_type=F32).astype(BF16)


def spread(block, axis, size, groups=None):
    return lax.all_to_all(
        jnp.broadcast_to(block[None], (size,) + block.shape), axis, 0, 0, axis_index_groups=groups
    )


def body(context, w_out, residual, w_proj, hidden, gain, matched):
    width = hidden.shape[1]
    own_rows = hidden.shape[0]
    c, x, zh = (lax.axis_index(name) for name in ("c", "x", "zh"))
    z = zh * NZL + lax.axis_index("zl")
    m = x * NZH + zh
    meta = jnp.stack([z, zh, m, c, x]).astype(jnp.int32)
    idx, idx_row = matched.reshape(8, 48, 1), matched.reshape(1, matched.shape[0])
    gain_row = gain.reshape(1, width)
    first = c == 0

    hid, normed = call(
        norm_rows,
        [((48, width), BF16), ((48, width), BF16)],
        [SMEM] + [VMEM] * 3,
        [],
        2 * 48 * 128 * width,
        2 << 20,
        "norm",
    )(meta, idx, hidden, gain_row)
    normed = lax.all_gather(normed, "x", axis=0, tiled=True)

    got = lax.ppermute(jnp.where(first, w_out, jnp.pad(w_proj, ((0, 8), (0, 0)))), "c", SWAP)
    (pair,) = call(
        pair_rows, [((8, 2, 64, 512), BF16)], [SMEM] + [VMEM] * 3, [], 0, 2 << 20, "pair"
    )(meta, got, w_proj, w_out)
    lines = lax.all_to_all(pair, AXES, 0, 0, axis_index_groups=Z_ON_0)
    (line,) = call(tighten, [((1024, 512), BF16)], [SMEM, VMEM], [], 0, 2 << 20, "tighten")(meta, lines)

    here, away = call(
        pick_rows, [((192, 1024), BF16)] * 2, [SMEM] + [VMEM] * 3, [], 2 * 384 * 128 * 1024, 3 << 20, "pick"
    )(meta, idx, context, residual)
    line, away, normed = lax.optimization_barrier((line, away, normed))
    w = lax.all_gather(line, AXES, axis=0, tiled=True, axis_index_groups=Y_ON_0).reshape(8, 1024, 512)

    heads, res_own = call(
        join, [((192, 1024), BF16)] * 2, [SMEM, VMEM, VMEM], [], 0, 3 << 20, "join"
    )(meta, here, lax.ppermute(away, "zh", SWAP))
    res_oth = lax.ppermute(res_own, AXES, [(dev(y, z, 1, x), dev(y, z, 0, x)) for y, z, x in CHIPS])

    heads = [heads] + [lax.ppermute(heads, "x", [(i, (i - d) % NX) for i in range(NX)]) for d in range(1, NX)]
    keep, give = call(
        choose, [((192, 4096), BF16)] * 2, [SMEM] + [VMEM] * 5, [], 0, 6 << 20, "choose"
    )(meta, normed, *heads)
    give, res_oth = lax.optimization_barrier((give, res_oth))
    taken = lax.ppermute(give, "c", SWAP)

    wbuf = [pltpu.VMEM((8, 1024, 512), BF16), pltpu.SemaphoreType.DMA((8,))]
    pred, teach = call(
        forward,
        [((384, 1024), F32), ((384, 1024), BF16)],
        [SMEM] + [VMEM] * 2 + [ANY],
        wbuf,
        2 * 384 * 4096 * 1024,
        13 << 20,
        "forward",
    )(meta, keep, taken, w)
    teach = lax.ppermute(teach, AXES, [(dev(y, z, 1, x), dev(y, z, 0, x)) for y, z, x in CHIPS])
    term_own, term_oth, gain_part = call(
        backward,
        [((192, width), BF16), ((192, width), BF16), ((1, width), F32)],
        [SMEM] + [VMEM] * 7 + [ANY],
        [pltpu.VMEM((384, 1024), BF16)] + wbuf,
        2 * 384 * width * 1024,
        16 << 20,
        "backward",
    )(meta, pred, teach, res_own, res_oth, keep, taken, gain_row, w)

    gain_wide = jnp.broadcast_to(gain_part.reshape(1, 28, 128), (16, 28, 128))
    gain_wide, term_oth = lax.optimization_barrier((gain_wide, term_oth))
    gain_part = jnp.sum(lax.all_to_all(gain_wide, AXES, 0, 0, axis_index_groups=FIRST), axis=0)

    handed = lax.ppermute(term_oth, AXES, [(dev(y, z, 0, x), dev(y, z, 1, x)) for y, z, x in CHIPS])
    summed = jnp.where(first, term_own, handed).reshape(NX, 48, width)
    parts = [lax.dynamic_index_in_dim(summed, (x + d) % NX, 0, keepdims=False) for d in range(NX)]
    gain_part, parts[0] = lax.optimization_barrier((gain_part, parts[0]))
    for d in range(1, NX):
        parts[d] = lax.ppermute(parts[d], "x", [(i, (i + d) % NX) for i in range(NX)])
    (grad_hidden,) = call(
        finish, [((own_rows, width), BF16)], [SMEM] + [VMEM] * 7, [], 1 << 36, 4 << 20, "finish"
    )(meta, idx_row, *parts, hid, gain_row)

    gain_part = jnp.sum(spread(gain_part, AXES, 16, SECOND), axis=0)
    grad_gain = (gain_part + lax.ppermute(gain_part, "c", SWAP)).reshape(width)
    gain_update = grad_gain * lax.rsqrt(jnp.mean(grad_gain * grad_gain) + EPS)
    return (grad_hidden, gain_update)


def solution(mesh):
    fine = Mesh(mesh.devices.reshape(NY, NZL, NC, NX, NZH), AXES)
    dp, mp = ("y", "zl", "c"), ("x", "zh")
    return jax.shard_map(
        body,
        mesh=fine,
        in_specs=(P(dp, mp), P(dp, mp), P(dp, mp), P(dp, mp), P(dp + mp, None), P(), P(dp)),
        out_specs=(P(dp + mp, None), P()),
        check_vma=False,
    )
```

```python
import jax
import jax.numpy as jnp
from jax import lax
from jax.experimental import pallas as pl
from jax.experimental.pallas import tpu as pltpu
from jax.sharding import Mesh
from jax.sharding import PartitionSpec as P

EPS = 1e-06
NY, NZL, NC, NX, NZH = 8, 4, 2, 4, 2
NZ = NZL * NZH
AXES = ("y", "zl", "c", "x", "zh")
F32 = jnp.float32
BF16 = jnp.bfloat16
NT = (((1,), (1,)), ((), ()))


def dev(y, z, c, x):
    return (((y * NZL + z % NZL) * NC + c) * NX + x) * NZH + z // NZL


CHIPS = [(y, z, x) for y in range(NY) for z in range(NZ) for x in range(NX)]
Z_ON_0 = [[dev(y, z, 0, x) for z in range(NZ)] for y in range(NY) for x in range(NX)] + [
    [dev(y, z, 1, x) for y in range(NY)] for z in range(NZ) for x in range(NX)
]
Y_ON_0 = [[dev(y, z, 0, x) for y in range(NY)] for z in range(NZ) for x in range(NX)] + [
    [dev(y, z, 1, x) for z in range(NZ)] for y in range(NY) for x in range(NX)
]
FIRST = [
    [dev(h * 4 + y, z, c, x) for x in range(NX) for y in range(4)]
    for h in range(2)
    for z in range(NZ)
    for c in range(NC)
]
SECOND = [
    [dev(h * 4 + y, z, c, x) for h in range(2) for z in range(NZ)]
    for c in range(NC)
    for x in range(NX)
    for y in range(4)
]
SWAP = [(0, 1), (1, 0)]
DOWN = [(dev(y, z, 0, x), dev(y, z, 1, x)) for y, z, x in CHIPS]
UP = [(b, a) for a, b in DOWN]

VMEM = pl.BlockSpec(memory_space=pltpu.VMEM)
SMEM = pl.BlockSpec(memory_space=pltpu.SMEM)
ANY = pl.BlockSpec(memory_space=pl.ANY)
PARAMS = pltpu.CompilerParams(vmem_limit_bytes=48 * 1024 * 1024)


def call(kernel, outs, ins, scratch, flops, nbytes, name):
    return pl.pallas_call(
        kernel,
        out_shape=[jax.ShapeDtypeStruct(shape, kind) for shape, kind in outs],
        in_specs=ins,
        out_specs=[VMEM] * len(outs),
        scratch_shapes=scratch,
        compiler_params=PARAMS,
        cost_estimate=pl.CostEstimate(flops=flops, bytes_accessed=nbytes, transcendentals=0),
        name=name,
    )


def hot_rows(idx, b):
    return (lax.broadcasted_iota(jnp.int32, (48, 128), 1) + b * 128 == idx[b]).astype(BF16)


def pick_rows(meta, idx, context, residual, mine, theirs):
    for b in range(8):
        x, zh = b // NZH, b % NZH
        hot = hot_rows(idx, b)
        for part, ref in enumerate((context, residual)):
            rows = jnp.dot(hot, ref[b * 128 : b * 128 + 128, :], preferred_element_type=F32).astype(BF16)
            at = (slice(x * 48, x * 48 + 48), slice(part * 512, part * 512 + 512))

            @pl.when(meta[1] == zh)
            def _():
                mine[at] = rows

            @pl.when(meta[1] != zh)
            def _():
                theirs[at] = rows


def norm_rows(meta, idx, hidden, gain, hid_out, normed_out):
    hid = jnp.dot(hot_rows(idx, meta[2]), hidden[...], preferred_element_type=F32)
    hid_out[...] = hid.astype(BF16)
    stat = lax.rsqrt(jnp.mean(hid * hid, axis=1, keepdims=True) + EPS)
    normed_out[...] = (hid * stat * gain[...]).astype(BF16)


def pair_rows(meta, got, proj, outp, out):
    @pl.when(meta[3] == 0)
    def _():
        for i in range(8):
            out[i, 0, :56, :] = proj[...]
            out[i, 0, 56:, :] = jnp.zeros((8, 512), BF16)
            out[i, 1] = got[...]

    @pl.when(meta[3] != 0)
    def _():
        for i in range(8):
            out[i, 0] = got[...]
            out[i, 1] = outp[...]


def tighten(meta, lines, out):
    @pl.when(meta[3] == 0)
    def _():
        for h in range(NZH):
            for i in range(8):
                row = h * 512 + i * 56
                out[row : row + 56, :] = lines[h * 4 + i // 2, i % 2, :56, :]
            out[h * 512 + 448 : h * 512 + 512, :] = jnp.zeros((64, 512), BF16)

    @pl.when(meta[3] != 0)
    def _():
        for i in range(16):
            out[i * 64 : i * 64 + 64, :] = lines[i // 2, i % 2]


def join(meta, here, other, heads, res):
    def put(zh, low, high):
        @pl.when(meta[1] == zh)
        def _():
            heads[:, :512], heads[:, 512:] = low[:, :512], high[:, :512]
            res[:, :512], res[:, 512:] = low[:, 512:], high[:, 512:]

    put(0, here, other)
    put(1, other, here)


def choose(meta, *refs):
    normed, heads, (keep, give) = refs[:NX], refs[NX : 2 * NX], refs[2 * NX :]

    def put(core, to_normed, to_heads):
        @pl.when(meta[3] == core)
        def _():
            for y in range(NY):
                to_normed[:, y * 512 + 448 : y * 512 + 512] = jnp.zeros((192, 64), BF16)
            for d in range(NX):
                x = (meta[4] + d) % NX
                rows = pl.ds(pl.multiple_of(x * 48, 16), 48)
                for y in range(NY):
                    to_normed[rows, y * 512 : y * 512 + 448] = normed[d][:, y * 448 : y * 448 + 448]
                to_heads[:, pl.ds(pl.multiple_of(x * 1024, 1024), 1024)] = heads[d][...]

    put(0, keep, give)
    put(1, give, keep)


def load(w, buf, sems):
    copies = [pltpu.make_async_copy(w.at[k], buf.at[k], sems.at[k]) for k in range(8)]
    for copy in copies:
        copy.start()
    return copies


def forward(meta, own, oth, w, out, teach, buf, sems):
    copies = load(w, buf, sems)
    out[...] = jnp.zeros_like(out)

    def part(lanes):
        pieces = [jnp.concatenate([ref[:, lane] for lane in lanes], axis=1) for ref in (own, oth)]
        return jnp.concatenate(pieces, axis=0)

    for k in range(8):
        copies[k].wait()

        @pl.when(meta[3] == 0)
        def _():
            a = part([slice(k * 512, k * 512 + 512)])
            for h in range(NZH):
                cols = slice(h * 512, h * 512 + 512)
                out[:, cols] += jnp.dot(a, buf[k, cols, :], preferred_element_type=F32)

        @pl.when(meta[3] != 0)
        def _():
            a = part([slice(y * 512 + k % NZL * 128, y * 512 + k % NZL * 128 + 128) for y in range(NY)])
            cols = slice(k // NZL * 512, k // NZL * 512 + 512)
            out[:, cols] += jnp.dot(a, buf[k], preferred_element_type=F32)

    teach[:192] = out[192:].astype(BF16)
    teach[192:] = out[:192].astype(BF16)


def backward(meta, pred, teach, res_own, res_oth, own, oth, gain, w, term_own, term_oth, gain_out, g_buf, buf, sems):
    copies = load(w, buf, sems)
    g_buf[:192] = (pred[:192] - (res_own[...].astype(F32) + teach[:192].astype(F32))).astype(BF16)
    g_buf[192:] = (pred[192:] - (res_oth[...].astype(F32) + teach[192:].astype(F32))).astype(BF16)
    for y in range(NY):
        copies[y].wait()
        cols = slice(y * 448, y * 448 + 448)
        lanes = slice(y * 512, y * 512 + 448)
        term = lax.dot_general(g_buf[:, :512], buf[y, :448, :], NT, preferred_element_type=F32)
        term = term + lax.dot_general(g_buf[:, 512:], buf[y, 512:960, :], NT, preferred_element_type=F32)
        a = jnp.concatenate([own[:, lanes], oth[:, lanes]], axis=0).astype(F32)
        gain_out[:, cols] = jnp.sum(term * a, axis=0, keepdims=True) / gain[:, cols]
        term = term.astype(BF16)
        term_own[:, cols] = term[:192]
        term_oth[:, cols] = term[192:]


def finish(meta, idx, summed, hid_ref, gain_ref, out):
    gain = gain_ref[...]
    hid = hid_ref[...].astype(F32)
    scaled = summed[...].astype(F32) * gain
    width = hid.shape[1]
    stat = lax.rsqrt(jnp.mean(hid * hid, axis=1, keepdims=True) + EPS)
    inner = jnp.sum(hid * scaled, axis=1, keepdims=True)
    rows = (stat * scaled - hid * (stat * stat * stat * inner / width)).astype(BF16)
    m = meta[2]
    own = idx[:, :48]
    for b in range(1, 8):
        own = jnp.where(m == b, idx[:, b * 48 : b * 48 + 48] - b * 128, own)
    hot = (lax.broadcasted_iota(jnp.int32, (128, 48), 0) == own).astype(BF16)
    out[...] = jnp.dot(hot, rows, preferred_element_type=F32).astype(BF16)


def spread(block, axis, size, groups=None):
    return lax.all_to_all(
        jnp.broadcast_to(block[None], (size,) + block.shape), axis, 0, 0, axis_index_groups=groups
    )


def body(context, w_out, residual, w_proj, hidden, gain, matched):
    width = hidden.shape[1]
    own_rows = hidden.shape[0]
    c, x, zh = (lax.axis_index(name) for name in ("c", "x", "zh"))
    z = zh * NZL + lax.axis_index("zl")
    m = x * NZH + zh
    meta = jnp.stack([z, zh, m, c, x]).astype(jnp.int32)
    idx, idx_row = matched.reshape(8, 48, 1), matched.reshape(1, matched.shape[0])
    gain_row = gain.reshape(1, width)
    first = c == 0

    hid, normed = call(
        norm_rows,
        [((48, width), BF16), ((48, width), BF16)],
        [SMEM] + [VMEM] * 3,
        [],
        2 * 48 * 128 * width,
        2 << 20,
        "norm",
    )(meta, idx, hidden, gain_row)

    got = lax.ppermute(jnp.where(first, w_out, jnp.pad(w_proj, ((0, 8), (0, 0)))), "c", SWAP)
    (pair,) = call(
        pair_rows, [((8, 2, 64, 512), BF16)], [SMEM] + [VMEM] * 3, [], 0, 2 << 20, "pair"
    )(meta, got, w_proj, w_out)
    lines = lax.all_to_all(pair, AXES, 0, 0, axis_index_groups=Z_ON_0)
    (line,) = call(tighten, [((1024, 512), BF16)], [SMEM, VMEM], [], 0, 2 << 20, "tighten")(meta, lines)

    here, away = call(
        pick_rows, [((192, 1024), BF16)] * 2, [SMEM] + [VMEM] * 3, [], 2 * 384 * 128 * 1024, 3 << 20, "pick"
    )(meta, idx, context, residual)
    line, away, normed = lax.optimization_barrier((line, away, normed))
    w = lax.all_gather(line, AXES, axis=0, tiled=True, axis_index_groups=Y_ON_0).reshape(8, 1024, 512)

    other = lax.ppermute(away, "zh", SWAP)

    def around(block):
        return [block] + [lax.ppermute(block, "x", [(i, (i - d) % NX) for i in range(NX)]) for d in range(1, NX)]

    normed = around(normed)
    heads, res_own = call(
        join, [((192, 1024), BF16)] * 2, [SMEM, VMEM, VMEM], [], 0, 3 << 20, "join"
    )(meta, here, other)
    res_oth = lax.ppermute(res_own, AXES, UP)

    keep, give = call(
        choose, [((192, 4096), BF16)] * 2, [SMEM] + [VMEM] * 8, [], 0, 6 << 20, "choose"
    )(meta, *normed, *around(heads))
    give, res_oth = lax.optimization_barrier((give, res_oth))
    taken = lax.ppermute(give, "c", SWAP)

    wbuf = [pltpu.VMEM((8, 1024, 512), BF16), pltpu.SemaphoreType.DMA((8,))]
    pred, teach = call(
        forward,
        [((384, 1024), F32), ((384, 1024), BF16)],
        [SMEM] + [VMEM] * 2 + [ANY],
        wbuf,
        2 * 384 * 4096 * 1024,
        13 << 20,
        "forward",
    )(meta, keep, taken, w)
    teach = lax.ppermute(teach, AXES, UP)
    term_own, term_oth, gain_part = call(
        backward,
        [((192, width), BF16), ((192, width), BF16), ((1, width), F32)],
        [SMEM] + [VMEM] * 7 + [ANY],
        [pltpu.VMEM((384, 1024), BF16)] + wbuf,
        2 * 384 * width * 1024,
        16 << 20,
        "backward",
    )(meta, pred, teach, res_own, res_oth, keep, taken, gain_row, w)

    gain_part = gain_part.reshape(28, 128)
    gain_part = jnp.where(first, gain_part, lax.ppermute(gain_part, AXES, DOWN))
    gain_wide = jnp.broadcast_to(gain_part[None], (16, 28, 128))
    gain_wide, handed = lax.optimization_barrier((gain_wide, lax.ppermute(term_oth, AXES, DOWN)))
    gain_part = jnp.sum(lax.all_to_all(gain_wide, AXES, 0, 0, axis_index_groups=FIRST), axis=0)

    summed = lax.psum_scatter(jnp.where(first, term_own, handed), "x", scatter_dimension=0, tiled=True)
    (grad_hidden,) = call(
        finish, [((own_rows, width), BF16)], [SMEM] + [VMEM] * 4, [], 2 * 128 * 48 * width, 4 << 20, "finish"
    )(meta, idx_row, summed, hid, gain_row)

    gathered, grad_hidden = lax.optimization_barrier((spread(gain_part, AXES, 16, SECOND), grad_hidden))
    grad_gain = jnp.sum(gathered, axis=0).reshape(width)
    gain_update = grad_gain * lax.rsqrt(jnp.mean(grad_gain * grad_gain) + EPS)
    return (grad_hidden, gain_update)


def solution(mesh):
    fine = Mesh(mesh.devices.reshape(NY, NZL, NC, NX, NZH), AXES)
    dp, mp = ("y", "zl", "c"), ("x", "zh")
    return jax.shard_map(
        body,
        mesh=fine,
        in_specs=(P(dp, mp), P(dp, mp), P(dp, mp), P(dp, mp), P(dp + mp, None), P(), P(dp)),
        out_specs=(P(dp + mp, None), P()),
        check_vma=False,
    )
```

```python
import jax
import jax.numpy as jnp
from jax import lax
from jax.experimental import pallas as pl
from jax.experimental.pallas import tpu as pltpu
from jax.sharding import Mesh
from jax.sharding import PartitionSpec as P

EPS = 1e-06
NY, NZL, NC, NX, NZH = 8, 4, 2, 4, 2
NZ = NZL * NZH
AXES = ("y", "zl", "c", "x", "zh")
F32 = jnp.float32
BF16 = jnp.bfloat16
NT = (((1,), (1,)), ((), ()))


def dev(y, z, c, x):
    return (((y * NZL + z % NZL) * NC + c) * NX + x) * NZH + z // NZL


CHIPS = [(y, z, x) for y in range(NY) for z in range(NZ) for x in range(NX)]
Z_ON_0 = [[dev(y, z, 0, x) for z in range(NZ)] for y in range(NY) for x in range(NX)] + [
    [dev(y, z, 1, x) for y in range(NY)] for z in range(NZ) for x in range(NX)
]
Y_ON_0 = [[dev(y, z, 0, x) for y in range(NY)] for z in range(NZ) for x in range(NX)] + [
    [dev(y, z, 1, x) for z in range(NZ)] for y in range(NY) for x in range(NX)
]
FIRST = [[dev(y, z, c, x) for x in range(NX) for y in range(NY)] for z in range(NZ) for c in range(NC)]
SECOND = [[dev(y, z, c, x) for z in range(NZ)] for c in range(NC) for x in range(NX) for y in range(NY)]
SWAP = [(0, 1), (1, 0)]
DOWN = [(dev(y, z, 0, x), dev(y, z, 1, x)) for y, z, x in CHIPS]
UP = [(b, a) for a, b in DOWN]

VMEM = pl.BlockSpec(memory_space=pltpu.VMEM)
SMEM = pl.BlockSpec(memory_space=pltpu.SMEM)
ANY = pl.BlockSpec(memory_space=pl.ANY)
PARAMS = pltpu.CompilerParams(vmem_limit_bytes=48 * 1024 * 1024)


def call(kernel, outs, ins, scratch, flops, nbytes, name):
    return pl.pallas_call(
        kernel,
        out_shape=[jax.ShapeDtypeStruct(shape, kind) for shape, kind in outs],
        in_specs=ins,
        out_specs=[VMEM] * len(outs),
        scratch_shapes=scratch,
        compiler_params=PARAMS,
        cost_estimate=pl.CostEstimate(flops=flops, bytes_accessed=nbytes, transcendentals=0),
        name=name,
    )


def hot_rows(idx, b):
    return (lax.broadcasted_iota(jnp.int32, (48, 128), 1) + b * 128 == idx[b]).astype(BF16)


def pick_rows(meta, idx, context, residual, mine, theirs):
    for b in range(8):
        x, zh = b // NZH, b % NZH
        hot = hot_rows(idx, b)
        for part, ref in enumerate((context, residual)):
            rows = jnp.dot(hot, ref[b * 128 : b * 128 + 128, :], preferred_element_type=F32).astype(BF16)
            at = (slice(x * 48, x * 48 + 48), slice(part * 512, part * 512 + 512))

            @pl.when(meta[1] == zh)
            def _():
                mine[at] = rows

            @pl.when(meta[1] != zh)
            def _():
                theirs[at] = rows


def norm_rows(meta, idx, hidden, gain, hid_out, normed_out):
    hid = jnp.dot(hot_rows(idx, meta[2]), hidden[...], preferred_element_type=F32)
    hid_out[...] = hid.astype(BF16)
    stat = lax.rsqrt(jnp.mean(hid * hid, axis=1, keepdims=True) + EPS)
    normed_out[...] = (hid * stat * gain[...]).astype(BF16)


def pair_rows(meta, got, proj, outp, out):
    @pl.when(meta[3] == 0)
    def _():
        for i in range(8):
            out[i, 0, :56, :] = proj[...]
            out[i, 0, 56:, :] = jnp.zeros((8, 512), BF16)
            out[i, 1] = got[...]

    @pl.when(meta[3] != 0)
    def _():
        for i in range(8):
            out[i, 0] = got[...]
            out[i, 1] = outp[...]


def tighten(meta, lines, out):
    @pl.when(meta[3] == 0)
    def _():
        for h in range(NZH):
            for i in range(8):
                row = h * 512 + i * 56
                out[row : row + 56, :] = lines[h * 4 + i // 2, i % 2, :56, :]
            out[h * 512 + 448 : h * 512 + 512, :] = jnp.zeros((64, 512), BF16)

    @pl.when(meta[3] != 0)
    def _():
        for i in range(16):
            out[i * 64 : i * 64 + 64, :] = lines[i // 2, i % 2]


def join(meta, here, other, heads, res):
    def put(zh, low, high):
        @pl.when(meta[1] == zh)
        def _():
            heads[:, :512], heads[:, 512:] = low[:, :512], high[:, :512]
            res[:, :512], res[:, 512:] = low[:, 512:], high[:, 512:]

    put(0, here, other)
    put(1, other, here)


def choose(meta, *refs):
    normed, heads, (keep, give) = refs[:NX], refs[NX : 2 * NX], refs[2 * NX :]

    def put(core, to_normed, to_heads):
        @pl.when(meta[3] == core)
        def _():
            for y in range(NY):
                to_normed[:, y * 512 + 448 : y * 512 + 512] = jnp.zeros((192, 64), BF16)
            for d in range(NX):
                x = (meta[4] + d) % NX
                rows = pl.ds(pl.multiple_of(x * 48, 16), 48)
                for y in range(NY):
                    to_normed[rows, y * 512 : y * 512 + 448] = normed[d][:, y * 448 : y * 448 + 448]
                to_heads[:, pl.ds(pl.multiple_of(x * 1024, 1024), 1024)] = heads[d][...]

    put(0, keep, give)
    put(1, give, keep)


def load(w, buf, sems):
    copies = [pltpu.make_async_copy(w.at[k], buf.at[k], sems.at[k]) for k in range(8)]
    for copy in copies:
        copy.start()
    return copies


def forward(meta, own, oth, w, out, teach, buf, sems):
    copies = load(w, buf, sems)
    out[...] = jnp.zeros_like(out)

    def part(lanes):
        pieces = [jnp.concatenate([ref[:, lane] for lane in lanes], axis=1) for ref in (own, oth)]
        return jnp.concatenate(pieces, axis=0)

    for k in range(8):
        copies[k].wait()

        @pl.when(meta[3] == 0)
        def _():
            a = part([slice(k * 512, k * 512 + 512)])
            for h in range(NZH):
                cols = slice(h * 512, h * 512 + 512)
                out[:, cols] += jnp.dot(a, buf[k, cols, :], preferred_element_type=F32)

        @pl.when(meta[3] != 0)
        def _():
            a = part([slice(y * 512 + k % NZL * 128, y * 512 + k % NZL * 128 + 128) for y in range(NY)])
            cols = slice(k // NZL * 512, k // NZL * 512 + 512)
            out[:, cols] += jnp.dot(a, buf[k], preferred_element_type=F32)

    teach[:192] = out[192:].astype(BF16)
    teach[192:] = out[:192].astype(BF16)


def backward(meta, pred, teach, res_own, res_oth, own, oth, gain, w, term_own, term_oth, gain_out, g_buf, buf, sems):
    copies = load(w, buf, sems)
    g_buf[:192] = (pred[:192] - (res_own[...].astype(F32) + teach[:192].astype(F32))).astype(BF16)
    g_buf[192:] = (pred[192:] - (res_oth[...].astype(F32) + teach[192:].astype(F32))).astype(BF16)
    for y in range(NY):
        copies[y].wait()
        cols = slice(y * 448, y * 448 + 448)
        lanes = slice(y * 512, y * 512 + 448)
        term = lax.dot_general(g_buf[:, :512], buf[y, :448, :], NT, preferred_element_type=F32)
        term = term + lax.dot_general(g_buf[:, 512:], buf[y, 512:960, :], NT, preferred_element_type=F32)
        a = jnp.concatenate([own[:, lanes], oth[:, lanes]], axis=0).astype(F32)
        gain_out[:, cols] = jnp.sum(term * a, axis=0, keepdims=True) / gain[:, cols]
        term = term.astype(BF16)
        term_own[:, cols] = term[:192]
        term_oth[:, cols] = term[192:]


def finish(meta, idx, summed, hid_ref, gain_ref, out):
    gain = gain_ref[...]
    hid = hid_ref[...].astype(F32)
    scaled = summed[...].astype(F32) * gain
    width = hid.shape[1]
    stat = lax.rsqrt(jnp.mean(hid * hid, axis=1, keepdims=True) + EPS)
    inner = jnp.sum(hid * scaled, axis=1, keepdims=True)
    rows = (stat * scaled - hid * (stat * stat * stat * inner / width)).astype(BF16)
    m = meta[2]
    own = idx[:, :48]
    for b in range(1, 8):
        own = jnp.where(m == b, idx[:, b * 48 : b * 48 + 48] - b * 128, own)
    hot = (lax.broadcasted_iota(jnp.int32, (128, 48), 0) == own).astype(BF16)
    out[...] = jnp.dot(hot, rows, preferred_element_type=F32).astype(BF16)


def spread(block, axis, size, groups=None):
    return lax.all_to_all(
        jnp.broadcast_to(block[None], (size,) + block.shape), axis, 0, 0, axis_index_groups=groups
    )


def body(context, w_out, residual, w_proj, hidden, gain, matched):
    width = hidden.shape[1]
    own_rows = hidden.shape[0]
    c, x, zh = (lax.axis_index(name) for name in ("c", "x", "zh"))
    z = zh * NZL + lax.axis_index("zl")
    m = x * NZH + zh
    meta = jnp.stack([z, zh, m, c, x]).astype(jnp.int32)
    idx, idx_row = matched.reshape(8, 48, 1), matched.reshape(1, matched.shape[0])
    gain_row = gain.reshape(1, width)
    first = c == 0

    hid, normed = call(
        norm_rows,
        [((48, width), BF16), ((48, width), BF16)],
        [SMEM] + [VMEM] * 3,
        [],
        2 * 48 * 128 * width,
        2 << 20,
        "norm",
    )(meta, idx, hidden, gain_row)

    got = lax.ppermute(jnp.where(first, w_out, jnp.pad(w_proj, ((0, 8), (0, 0)))), "c", SWAP)
    (pair,) = call(
        pair_rows, [((8, 2, 64, 512), BF16)], [SMEM] + [VMEM] * 3, [], 0, 2 << 20, "pair"
    )(meta, got, w_proj, w_out)
    lines = lax.all_to_all(pair, AXES, 0, 0, axis_index_groups=Z_ON_0)
    (line,) = call(tighten, [((1024, 512), BF16)], [SMEM, VMEM], [], 0, 2 << 20, "tighten")(meta, lines)

    here, away = call(
        pick_rows, [((192, 1024), BF16)] * 2, [SMEM] + [VMEM] * 3, [], 2 * 384 * 128 * 1024, 3 << 20, "pick"
    )(meta, idx, context, residual)
    line, away, normed = lax.optimization_barrier((line, away, normed))
    w = lax.all_gather(line, AXES, axis=0, tiled=True, axis_index_groups=Y_ON_0).reshape(8, 1024, 512)

    other = lax.ppermute(away, "zh", SWAP)

    def around(block):
        return [block] + [lax.ppermute(block, "x", [(i, (i - d) % NX) for i in range(NX)]) for d in range(1, NX)]

    normed = around(normed)
    heads, res_own = call(
        join, [((192, 1024), BF16)] * 2, [SMEM, VMEM, VMEM], [], 0, 3 << 20, "join"
    )(meta, here, other)
    res_oth = lax.ppermute(res_own, AXES, UP)

    keep, give = call(
        choose, [((192, 4096), BF16)] * 2, [SMEM] + [VMEM] * 8, [], 0, 6 << 20, "choose"
    )(meta, *normed, *around(heads))
    give, res_oth = lax.optimization_barrier((give, res_oth))
    taken = lax.ppermute(give, "c", SWAP)

    wbuf = [pltpu.VMEM((8, 1024, 512), BF16), pltpu.SemaphoreType.DMA((8,))]
    pred, teach = call(
        forward,
        [((384, 1024), F32), ((384, 1024), BF16)],
        [SMEM] + [VMEM] * 2 + [ANY],
        wbuf,
        2 * 384 * 4096 * 1024,
        13 << 20,
        "forward",
    )(meta, keep, taken, w)
    teach = lax.ppermute(teach, AXES, UP)
    term_own, term_oth, gain_part = call(
        backward,
        [((192, width), BF16), ((192, width), BF16), ((1, width), F32)],
        [SMEM] + [VMEM] * 7 + [ANY],
        [pltpu.VMEM((384, 1024), BF16)] + wbuf,
        2 * 384 * width * 1024,
        16 << 20,
        "backward",
    )(meta, pred, teach, res_own, res_oth, keep, taken, gain_row, w)

    gain_part = gain_part.reshape(28, 128)
    gain_part = jnp.where(first, gain_part, lax.ppermute(gain_part, AXES, DOWN))
    gain_wide = jnp.broadcast_to(gain_part[None], (32, 28, 128))
    gain_wide, handed = lax.optimization_barrier((gain_wide, lax.ppermute(term_oth, AXES, DOWN)))
    gain_part = jnp.sum(lax.all_to_all(gain_wide, AXES, 0, 0, axis_index_groups=FIRST), axis=0)

    summed = lax.psum_scatter(jnp.where(first, term_own, handed), "x", scatter_dimension=0, tiled=True)
    (grad_hidden,) = call(
        finish, [((own_rows, width), BF16)], [SMEM] + [VMEM] * 4, [], 2 * 128 * 48 * width, 4 << 20, "finish"
    )(meta, idx_row, summed, hid, gain_row)

    gathered, grad_hidden = lax.optimization_barrier((spread(gain_part, AXES, 8, SECOND), grad_hidden))
    grad_gain = jnp.sum(gathered, axis=0).reshape(width)
    gain_update = grad_gain * lax.rsqrt(jnp.mean(grad_gain * grad_gain) + EPS)
    return (grad_hidden, gain_update)


def solution(mesh):
    fine = Mesh(mesh.devices.reshape(NY, NZL, NC, NX, NZH), AXES)
    dp, mp = ("y", "zl", "c"), ("x", "zh")
    return jax.shard_map(
        body,
        mesh=fine,
        in_specs=(P(dp, mp), P(dp, mp), P(dp, mp), P(dp, mp), P(dp + mp, None), P(), P(dp)),
        out_specs=(P(dp + mp, None), P()),
        check_vma=False,
    )
```
